128 devices in a mesh: wa: 32 (over y, z, core), row: 4 (over x).
Axes of the slice: x: 4, y: 4, z: 4, core: 2. Of those that a mesh axis runs over, the one named last changes fastest.
Arguments:
- rhs: float32 [4096, 128], P(('wa', 'row')), may hold values from -6 to 6
- tiles0: float32 [4096, 5, 128, 128], P(('wa', 'row')), may hold values from -0.25 to 0.25
- diag0: float32 [4096, 128], P(('wa', 'row')), may hold values from 1.5 to 4.5
- cols0: int32 [4096, 4], P(('wa', 'row')), may hold values from 0 to 4095, as said below
- tiles1: float32 [1024, 5, 128, 128], P(('wa', 'row')), may hold values from -0.25 to 0.25
- diag1: float32 [1024, 128], P(('wa', 'row')), may hold values from 1.5 to 4.5
- cols1: int32 [1024, 4], P(('wa', 'row')), may hold values from 0 to 1023, as said below
- tiles2: float32 [16, 5, 128, 128], replicated, may hold values from -0.25 to 0.25
- diag2: float32 [16, 128], replicated, may hold values from 1.5 to 4.5
- cols2: int32 [16, 4], replicated, may hold values from 0 to 15
- interp0: float32 [4096, 128, 128], P(('wa', 'row')), may hold values from -0.5 to 0.5
- owner0: int32 [4096], P(('wa', 'row')), may hold values from 0 to 1023, as said below
- interp1: float32 [1024, 128, 128], P(('wa', 'row')), may hold values from -0.5 to 0.5
- owner1: int32 [1024], P(('wa', 'row')), may hold values from 0 to 15
Outputs:
- solution: float32 [4096, 128], P(('wa', 'row'))
- coarse_correction: float32 [1024, 128], P('wa')
- coarsest_correction: float32 [16, 128], replicated
The draws below stay inside these ranges and needn't reach their ends.
Inputs may be any that keep to these rules, and one draw needn't show every extreme that they name: cols0[i, k] lies within 32 of i; cols0[i, 0] lies exactly 32 away from i, on a side drawn per row, unless that leaves the level, where it is clipped to the level's end. cols1[j, k] lies within 32 of j; cols1[j, 0] lies exactly 32 away from j, on a side drawn per row, unless that leaves the level, where it is clipped to the level's end. owner0[i] lies between 32 * (i // 128) and that plus 32 - 1.
All inputs are finite; a program needn't handle non-finite values.
Results may differ from the reference program's by a relative error of at most 0.00021.
Values sent between devices are 32-bit elements; how exact they have to be, the bound alone decides.
A program may use at most 128 MiB of HBM per device.

```python
import jax
import jax.numpy as jnp
from jax import lax

TILE = 128
K = 5
KN = 4
R0 = 32
NB0 = 4096
NB1 = 1024
NB2 = 16
SWEEPS = 2


def near_columns(key, count, reach, width):
    first, second = jax.random.split(key)
    rows = jnp.arange(count, dtype=jnp.int32)
    offsets = jax.random.randint(first, (count, width), -reach, reach + 1)
    sides = jax.random.randint(second, (count,), 0, 2) * 2 - 1
    offsets = offsets.at[:, 0].set(sides * reach)
    return jnp.clip(rows[:, None] + offsets, 0, count - 1).astype(jnp.int32)


def draw_cols0(key, part):
    key = jax.random.fold_in(key, 11)
    return near_columns(key, NB0, R0, KN)


def draw_cols1(key, part):
    key = jax.random.fold_in(key, 23)
    return near_columns(key, NB1, R0, KN)


def draw_owner0(key, part):
    key = jax.random.fold_in(key, 37)
    rows = jnp.arange(NB0, dtype=jnp.int32)
    group_rows = NB0 // NB1 * R0
    picks = jax.random.randint(key, (NB0,), 0, R0)
    return (rows // group_rows * R0 + picks).astype(jnp.int32)


def with_ends(values, own_key, low, top_value):
    place = [jax.random.randint(jax.random.fold_in(own_key, axis), (), 0, length) for axis, length in enumerate(values.shape)]
    widest = values.shape.index(max(values.shape))
    neighbour = place[:widest] + [(place[widest] + 1) % values.shape[widest]] + place[widest + 1:]
    return values.at[tuple(place)].set(low).at[tuple(neighbour)].set(top_value)


def block_scale(key, shape, cuts, smallest, largest):
    gain, own = 1.0, jax.random.fold_in(key, 6)
    for position, blocks in cuts:
        heights = jnp.exp(jax.random.uniform(jax.random.fold_in(own, position), (blocks,), jnp.float32, smallest / len(cuts), largest / len(cuts)))
        gain = gain * jnp.repeat(heights, shape[position] // blocks).reshape([-1 if axis == position else 1 for axis in range(len(shape))])
    return gain


def bell_draw(own_key, dims, spread, bound, cuts=(), kind=jnp.bfloat16):
    loudness = block_scale(own_key, dims, cuts, -0.22, 0.18) if cuts else 1.0
    entries = jax.random.normal(own_key, dims, jnp.float32) * spread * loudness
    return jnp.minimum(jnp.maximum(entries, -bound), bound).astype(kind)


def setup_inputs(seed: int = 0) -> dict:
    streams_of = jax.random.split(jax.random.key(seed), 15)
    return {
        "rhs": bell_draw(streams_of[0], (NB0, TILE), 1.0, 6.0, ((0, 128),), jnp.float32),
        "tiles0": bell_draw(streams_of[1], (NB0, K, TILE, TILE), (K * TILE) ** -0.5, 0.25, ((0, 128),), jnp.float32),
        "diag0": jnp.clip(1.5 + 3.0 * jax.random.uniform(streams_of[2], (NB0, TILE), jnp.float32) ** block_scale(streams_of[2], (NB0, TILE), ((0, 128),), -0.2, 0.2), 1.5, 4.5),
        "cols0": draw_cols0(jax.random.fold_in(streams_of[14], 71), 0),
        "tiles1": bell_draw(streams_of[4], (NB1, K, TILE, TILE), (K * TILE) ** -0.5, 0.25, ((0, 128),), jnp.float32),
        "diag1": jnp.clip(1.5 + 3.0 * jax.random.uniform(streams_of[5], (NB1, TILE), jnp.float32) ** block_scale(streams_of[5], (NB1, TILE), ((0, 128),), -0.2, 0.2), 1.5, 4.5),
        "cols1": draw_cols1(jax.random.fold_in(streams_of[14], 71), 0),
        "tiles2": bell_draw(streams_of[7], (NB2, K, TILE, TILE), (K * TILE) ** -0.5, 0.25, (), jnp.float32),
        "diag2": jnp.clip(jax.random.uniform(streams_of[8], (NB2, TILE), jnp.float32, 1.5, 4.5), 1.5, 4.5),
        "cols2": with_ends(jax.random.randint(streams_of[9], (NB2, KN), 0, NB2), jax.random.fold_in(streams_of[9], 1), 0, NB2 - 1).astype(jnp.int32),
        "interp0": bell_draw(streams_of[10], (NB0, TILE, TILE), TILE ** -0.5, 0.5, ((0, 128),), jnp.float32),
        "owner0": draw_owner0(jax.random.fold_in(streams_of[14], 71), 0),
        "interp1": bell_draw(streams_of[12], (NB1, TILE, TILE), TILE ** -0.5, 0.5, ((0, 128),), jnp.float32),
        "owner1": with_ends(jax.random.randint(streams_of[13], (NB1,), 0, NB2), jax.random.fold_in(streams_of[13], 1), 0, NB2 - 1).astype(jnp.int32),
    }


relax = 0.8
highest = lax.Precision.HIGHEST


def level_apply(tiles, diag, cols, field):
    stacked = jnp.concatenate([field[:, None, :], field[cols]], axis=1)
    return diag * field + jnp.einsum('bkij,bkj->bi', tiles, stacked, precision=highest)


def inverse_diagonal(tiles, diag):
    return 1.0 / (diag + jnp.einsum('bii->bi', tiles[:, 0]))


def sweeps(tiles, diag, cols, inv, right, field):
    for sweep in range(SWEEPS):
        field = field + relax * (right - level_apply(tiles, diag, cols, field)) * inv
    return field


def reference(rhs, tiles0, diag0, cols0, tiles1, diag1, cols1, tiles2, diag2, cols2, interp0, owner0, interp1, owner1):
    inv0 = inverse_diagonal(tiles0, diag0)
    inv1 = inverse_diagonal(tiles1, diag1)
    inv2 = inverse_diagonal(tiles2, diag2)
    field0 = sweeps(tiles0, diag0, cols0, inv0, rhs, jnp.zeros_like(rhs))
    resid0 = rhs - level_apply(tiles0, diag0, cols0, field0)
    lifted0 = jnp.einsum('bij,bi->bj', interp0, resid0, precision=highest)
    right1 = jax.ops.segment_sum(lifted0, owner0, num_segments=NB1)
    field1 = sweeps(tiles1, diag1, cols1, inv1, right1, jnp.zeros_like(right1))
    resid1 = right1 - level_apply(tiles1, diag1, cols1, field1)
    lifted1 = jnp.einsum('bij,bi->bj', interp1, resid1, precision=highest)
    right2 = jax.ops.segment_sum(lifted1, owner1, num_segments=NB2)
    field2 = sweeps(tiles2, diag2, cols2, inv2, right2, jnp.zeros_like(right2))
    field1 = field1 + jnp.einsum('bij,bj->bi', interp1, field2[owner1], precision=highest)
    field1 = sweeps(tiles1, diag1, cols1, inv1, right1, field1)
    field0 = field0 + jnp.einsum('bij,bj->bi', interp0, field1[owner0], precision=highest)
    field0 = sweeps(tiles0, diag0, cols0, inv0, rhs, field0)
    return field0, field1, field2
```

```python
import functools

import jax
import jax.numpy as jnp
from jax import lax
from jax.experimental import pallas as pl
from jax.experimental.pallas import tpu as pltpu
from jax.sharding import PartitionSpec as P

MESH = pl.DeviceIdType.MESH
TILE = 128
KN = 4
R0 = 32
R1 = 8
NB2 = 16
ROWS = 4
RING = 128
relax = 0.8


def position():
    group, row = lax.axis_index("wa"), lax.axis_index("row")
    return group * ROWS + row, group, row


def along(device, offset, count):
    place = lax.rem(device + (offset + count), count)
    return lax.div(place, ROWS), lax.rem(place, ROWS)


def plane_peers(group, row, planes):
    plane, core = lax.div(group, 2), lax.rem(group, 2)
    return [(lax.rem(plane + step, planes) * 2 + core, row) for step in range(1, planes)]


def chip_line_peers(group, row):
    core = lax.rem(group, 2)
    out = []
    for step in range(1, 2 * ROWS):
        flip, shift = divmod(step, ROWS)
        out.append((group - core + lax.rem(core + flip, 2), lax.rem(row + shift, ROWS)))
    return out


def lane_sums(products):
    return jnp.sum(products, axis=1, keepdims=True)


def eye_mask():
    shape = (TILE, TILE)
    return lax.broadcasted_iota(jnp.int32, shape, 0) == lax.broadcasted_iota(jnp.int32, shape, 1)


def lanes():
    return lax.broadcasted_iota(jnp.int32, (TILE, TILE), 1)


def row_products(tiles, field, cols, own, b):
    last = field.shape[0] - 1
    total = tiles[b, 0] * field[pl.ds(own + b, 1), :]
    for k in range(KN):
        total = total + tiles[b, k + 1] * field[pl.ds(cols[b, k] & last, 1), :]
    return total


def level_apply(tiles, field, cols, own, count, unroll):
    lane = lanes()

    def step(b, columns):
        return jnp.where(lane == b, lane_sums(row_products(tiles, field, cols, own, b)), columns)

    columns = lax.fori_loop(0, count, step, jnp.zeros((TILE, TILE), jnp.float32), unroll=unroll)
    return columns.T[:count]


def prolong(interp, coarse, owner, count, unroll):
    lane, last = lanes(), coarse.shape[0] - 1

    def step(b, columns):
        products = interp[b] * coarse[pl.ds(owner[b] & last, 1), :]
        return jnp.where(lane == b, lane_sums(products), columns)

    columns = lax.fori_loop(0, count, step, jnp.zeros((TILE, TILE), jnp.float32), unroll=unroll)
    return columns.T[:count]


def restrict(tiles, field, cols, own, rest, interp, owner, count, targets, unroll):
    eye = eye_mask()
    place = lax.broadcasted_iota(jnp.int32, (targets, TILE), 0)

    def step(b, sums):
        products = row_products(tiles, field, cols, own, b)
        residual = lane_sums(jnp.where(eye, rest[pl.ds(b, 1), :], 0.0) - products)
        lifted = jnp.sum(interp[b] * residual, axis=0, keepdims=True)
        return sums + jnp.where(place == owner[b] & (targets - 1), lifted, 0.0)

    return lax.fori_loop(0, count, step, jnp.zeros((targets, TILE), jnp.float32), unroll=unroll)


def diagonals(tiles, out, count, unroll):
    eye = eye_mask()

    def step(b, carry):
        out[pl.ds(b, 1), :] = jnp.sum(jnp.where(eye, tiles[b, 0], 0.0), axis=0, keepdims=True)
        return carry

    lax.fori_loop(0, count, step, 0, unroll=unroll)


def kernel(
    groups,
    rhs_hbm, tiles0_hbm, diag0_hbm, cols0_hbm, tiles1_hbm, diag1_hbm, cols1_hbm,
    tiles2_hbm, diag2_hbm, cols2_hbm, interp0_hbm, owner0_hbm, interp1_hbm, owner1_hbm,
    out0, out1, out2,
    rhs, tiles0, diag0, cols0, tiles1, diag1, cols1,
    tiles2, diag2, cols2, interp0, owner0, interp1, owner1,
    scale0, scale1, scale2, rest0, rest1, field2,
    fine_a, fine_b, fine_c, fine_d, mid_s, mid_a, mid_b, mid_c, mid_d,
    partial, parts, near, far,
    load_sem, send_sem, recv_sem,
):
    devices = groups * ROWS
    planes = groups // 2
    device, group, row = position()
    core = lax.rem(group, 2)
    plane = lax.div(group, 2)

    base0 = pl.multiple_of(lax.rem(device * R0, RING), R0)
    base1 = pl.multiple_of(lax.rem(device * R1, RING), R1)
    own0, own1 = pl.ds(base0, R0), pl.ds(base1, R1)

    own_tiles = pl.ds(0, 1)
    other_tiles = pl.ds(1, KN)

    def load(index, source, target):
        return pltpu.make_async_copy(source, target, load_sem.at[index])

    first = [
        load(0, tiles0_hbm.at[:, own_tiles], tiles0.at[:, own_tiles]),
        load(1, diag0_hbm, diag0),
        load(2, rhs_hbm, rhs),
        load(3, tiles1_hbm.at[:, own_tiles], tiles1.at[:, own_tiles]),
        load(4, diag1_hbm, diag1),
    ]
    fine = [
        load(5, tiles0_hbm.at[:, other_tiles], tiles0.at[:, other_tiles]),
        load(6, cols0_hbm, cols0),
        load(7, interp0_hbm, interp0),
        load(8, owner0_hbm, owner0),
    ]
    middle = [
        load(9, tiles1_hbm.at[:, other_tiles], tiles1.at[:, other_tiles]),
        load(10, cols1_hbm, cols1),
        load(11, interp1_hbm, interp1),
        load(12, owner1_hbm, owner1),
    ]
    coarse = [
        load(13, tiles2_hbm, tiles2),
        load(14, diag2_hbm, diag2),
        load(15, cols2_hbm, cols2),
    ]
    for copy in first:
        copy.start()

    around = [
        (lax.rem(group + side + groups, groups), place) for side in (-1, 1) for place in range(ROWS)
    ]
    mates = [(group, lax.rem(row + step, ROWS)) for step in range(1, ROWS)]
    far_peers = plane_peers(group, row, planes)
    barrier = pltpu.get_barrier_semaphore()
    greeted = around + mates + far_peers
    for peer in greeted:
        pl.semaphore_signal(barrier, inc=1, device_id=peer, device_id_type=MESH)

    for copy in first:
        copy.wait()
    for copy in fine + middle + coarse:
        copy.start()

    def send(index, source, target, peer):
        pltpu.make_async_remote_copy(
            src_ref=source, dst_ref=target, send_sem=send_sem.at[index], recv_sem=recv_sem.at[index],
            device_id=peer, device_id_type=MESH,
        ).start()

    def arrivals(index, like):
        return pltpu.make_async_remote_copy(
            src_ref=like, dst_ref=like, send_sem=send_sem.at[index], recv_sem=recv_sem.at[index],
            device_id=mates[0], device_id_type=MESH,
        )

    def send_fine(index, field):
        own = field.at[own0]
        for step in (1, -1):
            send(index, own, own, along(device, step, devices))

    def send_middle(index, field):
        own = field.at[own1]
        for step in (4, -4, 3, -3, 2, -2, 1, -1):
            send(index, own, own, along(device, step, devices))

    def fine_wait(index, field):
        arrivals(index, field.at[pl.ds(0, 2 * R0)]).wait_recv()

    def middle_wait(index, field):
        arrivals(index, field.at[pl.ds(0, 2 * R0)]).wait_recv()

    diagonals(tiles0, scale0, R0, 4)
    scale0[...] = relax / (diag0[...] + scale0[...])
    fine_a[own0, :] = rhs[...] * scale0[...]
    diagonals(tiles1, scale1, R1, 4)
    mid_s[own1, :] = relax / (diag1[...] + scale1[...])
    pl.semaphore_wait(barrier, len(greeted))
    send_fine(0, fine_a)
    send_middle(1, mid_s)

    def apply0(field):
        return level_apply(tiles0, field, cols0, base0, R0, 4)

    def sweep0(field):
        v = field[own0, :]
        return v + scale0[...] * (rhs[...] - diag0[...] * v - apply0(field))

    for copy in fine:
        copy.wait()
    fine_wait(0, fine_a)
    fine_b[own0, :] = sweep0(fine_a)
    send_fine(2, fine_b)
    rest0[...] = rhs[...] - diag0[...] * fine_b[own0, :]
    fine_wait(2, fine_b)
    part = restrict(tiles0, fine_b, cols0, base0, rest0, interp0, owner0, R0, R0, 4)

    partial[...] = part
    slot = row * (3 * R0)
    parts[pl.ds(slot + R0, R0), :] = part
    for place in range(ROWS):
        low = R1 * place
        send(3, partial.at[pl.ds(low, R0 - low)], parts.at[pl.ds(slot + low, R0 - low)],
             (lax.rem(group + 1, groups), place))
        send(3, partial.at[pl.ds(0, low + R1)], parts.at[pl.ds(slot + 2 * R0, low + R1)],
             (lax.rem(group + groups - 1, groups), place))
    for mate in mates:
        send(3, partial, parts.at[pl.ds(slot + R0, R0)], mate)
    for copy in middle:
        copy.wait()
    middle_wait(1, mid_s)
    arrivals(3, parts.at[pl.ds(0, 8 * R0)]).wait_recv()
    for block in range(2 * ROWS + 1):
        offset = (row + block) * R1
        right = parts[pl.ds(offset, R1), :]
        for place in range(1, ROWS):
            right = right + parts[pl.ds(offset + place * 3 * R0, R1), :]
        there = pl.ds(pl.multiple_of(lax.rem((device + (devices + block - ROWS)) * R1, RING), R1), R1)
        mid_a[there, :] = right * mid_s[there, :]
        if block == ROWS:
            right1 = right
    s1 = mid_s[own1, :]

    def sweep1(field):
        v = field[own1, :]
        return v + s1 * (right1 - diag1[...] * v - level_apply(tiles1, field, cols1, base1, R1, 4))

    mid_b[own1, :] = sweep1(mid_a)
    send_middle(4, mid_b)
    rest1[...] = right1 - diag1[...] * mid_b[own1, :]
    middle_wait(4, mid_b)
    part2 = restrict(tiles1, mid_b, cols1, base1, rest1, interp1, owner1, R1, NB2, 4)

    line_slot = core * ROWS + row
    near[line_slot] = part2
    for peer in chip_line_peers(group, row):
        send(5, near.at[line_slot], near.at[line_slot], peer)
    for copy in coarse:
        copy.wait()
    diagonals(tiles2, scale2, NB2, 4)
    scale2[...] = relax / (diag2[...] + scale2[...])
    arrivals(5, near.at[pl.ds(0, 2 * ROWS - 1)]).wait_recv()
    total = near[0]
    for place in range(1, 2 * ROWS):
        total = total + near[place]
    far[plane] = total
    for peer in far_peers:
        send(6, far.at[plane], far.at[plane], peer)
    arrivals(6, far.at[pl.ds(0, planes - 1)]).wait_recv()
    right2 = far[0]
    for place in range(1, planes):
        right2 = right2 + far[place]

    v2 = right2 * scale2[...]
    field2[...] = v2
    v2 = v2 + scale2[...] * (right2 - diag2[...] * v2 - level_apply(tiles2, field2, cols2, 0, NB2, 4))
    out2[...] = v2

    mid_c[own1, :] = mid_b[own1, :] + prolong(interp1, out2, owner1, R1, 4)
    send_middle(7, mid_c)
    middle_wait(7, mid_c)
    mid_d[own1, :] = sweep1(mid_c)
    send_middle(8, mid_d)
    middle_wait(8, mid_d)
    place1 = pl.ds(row * R1, R1)
    out1[place1, :] = sweep1(mid_d)
    for mate in mates:
        send(9, out1.at[place1], out1.at[place1], mate)
    arrivals(9, out1.at[pl.ds(0, R0 - R1)]).wait_recv()

    fine_c[own0, :] = fine_b[own0, :] + prolong(interp0, out1, owner0, R0, 4)
    send_fine(10, fine_c)
    fine_wait(10, fine_c)
    fine_d[own0, :] = sweep0(fine_c)
    send_fine(11, fine_d)
    fine_wait(11, fine_d)
    out0[...] = sweep0(fine_d)

    for index, like in (
        (0, fine_a.at[pl.ds(0, 2 * R0)]), (1, mid_s.at[pl.ds(0, 2 * R0)]), (2, fine_b.at[pl.ds(0, 2 * R0)]),
        (3, parts.at[pl.ds(0, 8 * R0)]), (4, mid_b.at[pl.ds(0, 2 * R0)]), (5, near.at[pl.ds(0, 2 * ROWS - 1)]),
        (6, far.at[pl.ds(0, planes - 1)]), (7, mid_c.at[pl.ds(0, 2 * R0)]), (8, mid_d.at[pl.ds(0, 2 * R0)]),
        (9, out1.at[pl.ds(0, R0 - R1)]), (10, fine_c.at[pl.ds(0, 2 * R0)]), (11, fine_d.at[pl.ds(0, 2 * R0)]),
    ):
        arrivals(index, like).wait_send()


def shards(groups, *arguments):
    f32 = jnp.float32
    vmem = lambda *shape: pltpu.VMEM(shape, f32)
    copies = []
    for index, argument in enumerate(arguments):
        space = pltpu.SMEM if argument.dtype == jnp.int32 else pltpu.VMEM
        copies.append(space(argument.shape, argument.dtype))
    scratch = copies + [
        vmem(R0, TILE), vmem(R1, TILE), vmem(NB2, TILE), vmem(R0, TILE), vmem(R1, TILE), vmem(NB2, TILE),
        *(vmem(RING, TILE) for _ in range(9)),
        vmem(R0, TILE), vmem(ROWS * 3 * R0, TILE), vmem(2 * ROWS, NB2, TILE), vmem(groups // 2, NB2, TILE),
        pltpu.SemaphoreType.DMA((16,)), pltpu.SemaphoreType.DMA((12,)), pltpu.SemaphoreType.DMA((12,)),
    ]
    return pl.pallas_call(
        functools.partial(kernel, groups),
        out_shape=tuple(jax.ShapeDtypeStruct((n, TILE), f32) for n in (R0, R0, NB2)),
        in_specs=[pl.BlockSpec(memory_space=pl.ANY)] * len(arguments),
        out_specs=(pl.BlockSpec(memory_space=pltpu.VMEM),) * 3,
        scratch_shapes=scratch,
        compiler_params=pltpu.CompilerParams(
            collective_id=0, has_side_effects=True, vmem_limit_bytes=56 * 2**20
        ),
        name="vcycle",
    )(*arguments)


def solution(mesh):
    both = ("wa", "row")
    in_specs = (
        P(both, None),
        P(both, None, None, None),
        P(both, None),
        P(both, None),
        P(both, None, None, None),
        P(both, None),
        P(both, None),
        P(),
        P(),
        P(),
        P(both, None, None),
        P(both),
        P(both, None, None),
        P(both),
    )
    out_specs = (P(both, None), P("wa", None), P())
    return jax.shard_map(
        functools.partial(shards, mesh.shape["wa"]), mesh=mesh, in_specs=in_specs, out_specs=out_specs, check_vma=False
    )
```

```python
import functools

import jax
import jax.numpy as jnp
from jax import lax
from jax.experimental import pallas as pl
from jax.experimental.pallas import tpu as pltpu
from jax.sharding import PartitionSpec as P

MESH = pl.DeviceIdType.MESH
TILE = 128
KN = 4
R0 = 32
R1 = 8
NB2 = 16
ROWS = 4
RING = 128
relax = 0.8


def position():
    group, row = lax.axis_index("wa"), lax.axis_index("row")
    return group * ROWS + row, group, row


def along(device, offset, count):
    place = lax.rem(device + (offset + count), count)
    return lax.div(place, ROWS), lax.rem(place, ROWS)


def plane_peers(group, row, planes):
    plane, core = lax.div(group, 2), lax.rem(group, 2)
    return [(lax.rem(plane + step, planes) * 2 + core, row) for step in range(1, planes)]


def chip_line_peers(group, row):
    core = lax.rem(group, 2)
    out = []
    for step in range(1, 2 * ROWS):
        flip, shift = divmod(step, ROWS)
        out.append((group - core + lax.rem(core + flip, 2), lax.rem(row + shift, ROWS)))
    return out


def lane_sums(products):
    return jnp.sum(products, axis=1, keepdims=True)


def eye_mask():
    shape = (TILE, TILE)
    return lax.broadcasted_iota(jnp.int32, shape, 0) == lax.broadcasted_iota(jnp.int32, shape, 1)


def lanes():
    return lax.broadcasted_iota(jnp.int32, (TILE, TILE), 1)


def row_products(tiles, field, cols, own, b):
    last = field.shape[0] - 1
    total = tiles[b, 0] * field[pl.ds(own + b, 1), :]
    for k in range(KN):
        total = total + tiles[b, k + 1] * field[pl.ds(cols[k, b] & last, 1), :]
    return total


def level_apply(tiles, field, cols, own, count, unroll):
    lane = lanes()

    def step(b, columns):
        return jnp.where(lane == b, lane_sums(row_products(tiles, field, cols, own, b)), columns)

    columns = lax.fori_loop(0, count, step, jnp.zeros((TILE, TILE), jnp.float32), unroll=unroll)
    return columns.T[:count]


def prolong(interp, coarse, owner, count, unroll):
    lane, last = lanes(), coarse.shape[0] - 1

    def step(b, columns):
        products = interp[b] * coarse[pl.ds(owner[b] & last, 1), :]
        return jnp.where(lane == b, lane_sums(products), columns)

    columns = lax.fori_loop(0, count, step, jnp.zeros((TILE, TILE), jnp.float32), unroll=unroll)
    return columns.T[:count]


def restrict(tiles, field, cols, own, rest, interp, owner, count, targets, unroll):
    eye = eye_mask()
    place = lax.broadcasted_iota(jnp.int32, (targets, TILE), 0)

    def step(b, sums):
        products = row_products(tiles, field, cols, own, b)
        residual = lane_sums(jnp.where(eye, rest[pl.ds(b, 1), :], 0.0) - products)
        lifted = jnp.sum(interp[b] * residual, axis=0, keepdims=True)
        return sums + jnp.where(place == owner[b] & (targets - 1), lifted, 0.0)

    return lax.fori_loop(0, count, step, jnp.zeros((targets, TILE), jnp.float32), unroll=unroll)


def diagonals(tiles, out, count, unroll):
    eye = eye_mask()

    def step(b, carry):
        out[pl.ds(b, 1), :] = jnp.sum(jnp.where(eye, tiles[b, 0], 0.0), axis=0, keepdims=True)
        return carry

    lax.fori_loop(0, count, step, 0, unroll=unroll)


def kernel(
    groups,
    rhs_hbm, tiles0_hbm, diag0_hbm, cols0_hbm, tiles1_hbm, diag1_hbm, cols1_hbm,
    tiles2_hbm, diag2_hbm, cols2_hbm, interp0_hbm, owner0_hbm, interp1_hbm, owner1_hbm,
    out0, out1, out2,
    rhs, tiles0, diag0, cols0, tiles1, diag1, cols1,
    tiles2, diag2, cols2, interp0, owner0, interp1, owner1,
    scale0, scale1, scale2, rest0, rest1, field2,
    fine_a, fine_b, fine_c, fine_d, mid_s, mid_a, mid_b, mid_c, mid_d,
    partial, parts, near, far,
    load_sem, send_sem, recv_sem,
):
    devices = groups * ROWS
    planes = groups // 2
    device, group, row = position()
    core = lax.rem(group, 2)
    plane = lax.div(group, 2)

    base0 = pl.multiple_of(lax.rem(device * R0, RING), R0)
    base1 = pl.multiple_of(lax.rem(device * R1, RING), R1)
    own0, own1 = pl.ds(base0, R0), pl.ds(base1, R1)

    own_tiles = pl.ds(0, 1)
    other_tiles = pl.ds(1, KN)

    def load(index, source, target):
        return pltpu.make_async_copy(source, target, load_sem.at[index])

    first = [
        load(0, tiles0_hbm.at[:, own_tiles], tiles0.at[:, own_tiles]),
        load(1, diag0_hbm, diag0),
        load(2, rhs_hbm, rhs),
    ]
    fine = [
        load(3, cols0_hbm, cols0),
        load(4, tiles0_hbm.at[:, other_tiles], tiles0.at[:, other_tiles]),
    ]
    middle = [
        load(5, tiles1_hbm, tiles1),
        load(6, diag1_hbm, diag1),
        load(7, cols1_hbm, cols1),
        load(8, interp0_hbm, interp0),
        load(9, owner0_hbm, owner0),
    ]
    coarse = [
        load(10, interp1_hbm, interp1),
        load(11, owner1_hbm, owner1),
        load(12, tiles2_hbm, tiles2),
        load(13, diag2_hbm, diag2),
        load(14, cols2_hbm, cols2),
    ]
    for copy in first:
        copy.start()

    around = [
        (lax.rem(group + side + groups, groups), place) for side in (-1, 1) for place in range(ROWS)
    ]
    mates = [(group, lax.rem(row + step, ROWS)) for step in range(1, ROWS)]
    far_peers = plane_peers(group, row, planes)
    barrier = pltpu.get_barrier_semaphore()
    greeted = around + mates + far_peers
    for peer in greeted:
        pl.semaphore_signal(barrier, inc=1, device_id=peer, device_id_type=MESH)

    for copy in first:
        copy.wait()
    for copy in fine:
        copy.start()

    def send(index, source, target, peer):
        pltpu.make_async_remote_copy(
            src_ref=source, dst_ref=target, send_sem=send_sem.at[index], recv_sem=recv_sem.at[index],
            device_id=peer, device_id_type=MESH,
        ).start()

    def arrivals(index, like):
        return pltpu.make_async_remote_copy(
            src_ref=like, dst_ref=like, send_sem=send_sem.at[index], recv_sem=recv_sem.at[index],
            device_id=mates[0], device_id_type=MESH,
        )

    def send_fine(index, field):
        own = field.at[own0]
        for step in (1, -1):
            send(index, own, own, along(device, step, devices))

    def send_middle(index, field):
        own = field.at[own1]
        for step in (4, -4, 3, -3, 2, -2, 1, -1):
            send(index, own, own, along(device, step, devices))

    def fine_wait(index, field):
        arrivals(index, field.at[pl.ds(0, 2 * R0)]).wait_recv()

    def middle_wait(index, field):
        arrivals(index, field.at[pl.ds(0, 2 * R0)]).wait_recv()

    diagonals(tiles0, scale0, R0, 4)
    scale0[...] = relax / (diag0[...] + scale0[...])
    fine_a[own0, :] = rhs[...] * scale0[...]
    pl.semaphore_wait(barrier, len(greeted))
    send_fine(0, fine_a)

    def apply0(field):
        return level_apply(tiles0, field, cols0, base0, R0, 16)

    def sweep0(field):
        v = field[own0, :]
        return v + scale0[...] * (rhs[...] - diag0[...] * v - apply0(field))

    for copy in fine:
        copy.wait()
    for copy in middle + coarse:
        copy.start()
    fine_wait(0, fine_a)
    fine_b[own0, :] = sweep0(fine_a)
    send_fine(2, fine_b)
    rest0[...] = rhs[...] - diag0[...] * fine_b[own0, :]
    for copy in middle:
        copy.wait()
    diagonals(tiles1, scale1, R1, 8)
    mid_s[own1, :] = relax / (diag1[...] + scale1[...])
    send_middle(1, mid_s)
    fine_wait(2, fine_b)
    part = restrict(tiles0, fine_b, cols0, base0, rest0, interp0, owner0, R0, R0, 8)

    partial[...] = part
    slot = row * (3 * R0)
    parts[pl.ds(slot + R0, R0), :] = part
    for place in range(ROWS):
        low = R1 * place
        send(3, partial.at[pl.ds(low, R0 - low)], parts.at[pl.ds(slot + low, R0 - low)],
             (lax.rem(group + 1, groups), place))
        send(3, partial.at[pl.ds(0, low + R1)], parts.at[pl.ds(slot + 2 * R0, low + R1)],
             (lax.rem(group + groups - 1, groups), place))
    for mate in mates:
        send(3, partial, parts.at[pl.ds(slot + R0, R0)], mate)
    middle_wait(1, mid_s)
    arrivals(3, parts.at[pl.ds(0, 8 * R0)]).wait_recv()
    for block in range(2 * ROWS + 1):
        offset = (row + block) * R1
        right = parts[pl.ds(offset, R1), :]
        for place in range(1, ROWS):
            right = right + parts[pl.ds(offset + place * 3 * R0, R1), :]
        there = pl.ds(pl.multiple_of(lax.rem((device + (devices + block - ROWS)) * R1, RING), R1), R1)
        mid_a[there, :] = right * mid_s[there, :]
        if block == ROWS:
            right1 = right
    s1 = mid_s[own1, :]

    def sweep1(field):
        v = field[own1, :]
        return v + s1 * (right1 - diag1[...] * v - level_apply(tiles1, field, cols1, base1, R1, 8))

    mid_b[own1, :] = sweep1(mid_a)
    send_middle(4, mid_b)
    rest1[...] = right1 - diag1[...] * mid_b[own1, :]
    for copy in coarse:
        copy.wait()
    diagonals(tiles2, scale2, NB2, 8)
    scale2[...] = relax / (diag2[...] + scale2[...])
    middle_wait(4, mid_b)
    part2 = restrict(tiles1, mid_b, cols1, base1, rest1, interp1, owner1, R1, NB2, 8)

    line_slot = core * ROWS + row
    near[line_slot] = part2
    for peer in chip_line_peers(group, row):
        send(5, near.at[line_slot], near.at[line_slot], peer)
    arrivals(5, near.at[pl.ds(0, 2 * ROWS - 1)]).wait_recv()
    total = near[0]
    for place in range(1, 2 * ROWS):
        total = total + near[place]
    far[plane] = total
    for peer in far_peers:
        send(6, far.at[plane], far.at[plane], peer)
    arrivals(6, far.at[pl.ds(0, planes - 1)]).wait_recv()
    right2 = far[0]
    for place in range(1, planes):
        right2 = right2 + far[place]

    v2 = right2 * scale2[...]
    field2[...] = v2
    v2 = v2 + scale2[...] * (right2 - diag2[...] * v2 - level_apply(tiles2, field2, cols2, 0, NB2, 16))
    out2[...] = v2

    mid_c[own1, :] = mid_b[own1, :] + prolong(interp1, out2, owner1, R1, 8)
    send_middle(7, mid_c)
    middle_wait(7, mid_c)
    mid_d[own1, :] = sweep1(mid_c)
    send_middle(8, mid_d)
    middle_wait(8, mid_d)
    place1 = pl.ds(row * R1, R1)
    out1[place1, :] = sweep1(mid_d)
    for mate in mates:
        send(9, out1.at[place1], out1.at[place1], mate)
    arrivals(9, out1.at[pl.ds(0, R0 - R1)]).wait_recv()

    fine_c[own0, :] = fine_b[own0, :] + prolong(interp0, out1, owner0, R0, 16)
    send_fine(10, fine_c)
    fine_wait(10, fine_c)
    fine_d[own0, :] = sweep0(fine_c)
    send_fine(11, fine_d)
    fine_wait(11, fine_d)
    out0[...] = sweep0(fine_d)

    for index, like in (
        (0, fine_a.at[pl.ds(0, 2 * R0)]), (1, mid_s.at[pl.ds(0, 2 * R0)]), (2, fine_b.at[pl.ds(0, 2 * R0)]),
        (3, parts.at[pl.ds(0, 8 * R0)]), (4, mid_b.at[pl.ds(0, 2 * R0)]), (5, near.at[pl.ds(0, 2 * ROWS - 1)]),
        (6, far.at[pl.ds(0, planes - 1)]), (7, mid_c.at[pl.ds(0, 2 * R0)]), (8, mid_d.at[pl.ds(0, 2 * R0)]),
        (9, out1.at[pl.ds(0, R0 - R1)]), (10, fine_c.at[pl.ds(0, 2 * R0)]), (11, fine_d.at[pl.ds(0, 2 * R0)]),
    ):
        arrivals(index, like).wait_send()


def hand_over(*refs):
    sources, targets, sems = refs[:3], refs[3:6], refs[6]
    copies = [pltpu.make_async_copy(sources[i], targets[i], sems.at[i]) for i in range(3)]
    for copy in copies:
        copy.start()
    for copy in copies:
        copy.wait()


def shards(groups, *arguments):
    f32 = jnp.float32
    arguments = [a.T if a.dtype == jnp.int32 and a.ndim == 2 else a for a in arguments]
    vmem = lambda *shape: pltpu.VMEM(shape, f32)
    copies = []
    for index, argument in enumerate(arguments):
        space = pltpu.SMEM if argument.dtype == jnp.int32 else pltpu.VMEM
        copies.append(space(argument.shape, argument.dtype))
    scratch = copies + [
        vmem(R0, TILE), vmem(R1, TILE), vmem(NB2, TILE), vmem(R0, TILE), vmem(R1, TILE), vmem(NB2, TILE),
        *(vmem(RING, TILE) for _ in range(9)),
        vmem(R0, TILE), vmem(ROWS * 3 * R0, TILE), vmem(2 * ROWS, NB2, TILE), vmem(groups // 2, NB2, TILE),
        pltpu.SemaphoreType.DMA((16,)), pltpu.SemaphoreType.DMA((12,)), pltpu.SemaphoreType.DMA((12,)),
    ]
    out_shape = tuple(jax.ShapeDtypeStruct((n, TILE), f32) for n in (R0, R0, NB2))
    results = pl.pallas_call(
        functools.partial(kernel, groups),
        out_shape=out_shape,
        in_specs=[pl.BlockSpec(memory_space=pl.ANY)] * len(arguments),
        out_specs=(pl.BlockSpec(memory_space=pltpu.VMEM),) * 3,
        scratch_shapes=scratch,
        compiler_params=pltpu.CompilerParams(
            collective_id=0, has_side_effects=True, vmem_limit_bytes=56 * 2**20
        ),
        name="vcycle",
    )(*arguments)
    return pl.pallas_call(
        hand_over,
        out_shape=out_shape,
        in_specs=[pl.BlockSpec(memory_space=pltpu.HBM)] * 3,
        out_specs=(pl.BlockSpec(memory_space=pltpu.HBM),) * 3,
        scratch_shapes=[pltpu.SemaphoreType.DMA((3,))],
        name="results",
    )(*results)


def solution(mesh):
    both = ("wa", "row")
    in_specs = (
        P(both, None),
        P(both, None, None, None),
        P(both, None),
        P(both, None),
        P(both, None, None, None),
        P(both, None),
        P(both, None),
        P(),
        P(),
        P(),
        P(both, None, None),
        P(both),
        P(both, None, None),
        P(both),
    )
    out_specs = (P(both, None), P("wa", None), P())
    return jax.shard_map(
        functools.partial(shards, mesh.shape["wa"]), mesh=mesh, in_specs=in_specs, out_specs=out_specs, check_vma=False
    )
```

```python
import functools

import jax
import jax.numpy as jnp
from jax import lax
from jax.experimental import pallas as pl
from jax.experimental.pallas import tpu as pltpu
from jax.sharding import PartitionSpec as P

MESH = pl.DeviceIdType.MESH
TILE = 128
KN = 4
R0 = 32
R1 = 8
NB2 = 16
ROWS = 4
RING = 128
relax = 0.8


def position():
    group, row = lax.axis_index("wa"), lax.axis_index("row")
    return group * ROWS + row, group, row


def along(device, offset, count):
    place = lax.rem(device + (offset + count), count)
    return lax.div(place, ROWS), lax.rem(place, ROWS)


STEPS = (4, -4, 3, -3, 2, -2, 1, -1)


def plane_peers(group, row, planes):
    plane, core = lax.div(group, 2), lax.rem(group, 2)
    return [(lax.rem(plane + step, planes) * 2 + core, row) for step in range(1, planes)]


def chip_line_peers(group, row):
    core = lax.rem(group, 2)
    out = []
    for step in range(1, 2 * ROWS):
        flip, shift = divmod(step, ROWS)
        out.append((group - core + lax.rem(core + flip, 2), lax.rem(row + shift, ROWS)))
    return out


def lane_sums(products):
    return jnp.sum(products, axis=1, keepdims=True)


def eye_mask():
    shape = (TILE, TILE)
    return lax.broadcasted_iota(jnp.int32, shape, 0) == lax.broadcasted_iota(jnp.int32, shape, 1)


def lanes():
    return lax.broadcasted_iota(jnp.int32, (TILE, TILE), 1)


def block_rows(products, count, unroll):
    lane = lanes()

    def step(b, columns):
        return jnp.where(lane == b, lane_sums(products(b)), columns)

    columns = lax.fori_loop(0, count, step, jnp.zeros((TILE, TILE), jnp.float32), unroll=unroll)
    return columns.T[:count]


def own_products(tiles, field, own):
    return lambda b: tiles[b, 0] * field[pl.ds(own + b, 1), :]


def neighbour_products(tiles, field, cols):
    last = field.shape[0] - 1

    def products(b):
        total = tiles[b, 1] * field[pl.ds(cols[0, b] & last, 1), :]
        for k in range(1, KN):
            total = total + tiles[b, k + 1] * field[pl.ds(cols[k, b] & last, 1), :]
        return total

    return products


def all_products(tiles, field, cols, own):
    mine, others = own_products(tiles, field, own), neighbour_products(tiles, field, cols)
    return lambda b: mine(b) + others(b)


def prolong(interp, coarse, owner, count, unroll):
    last = coarse.shape[0] - 1
    return block_rows(lambda b: interp[b] * coarse[pl.ds(owner[b] & last, 1), :], count, unroll)


def restrict(products_of, rest, interp, owner, count, targets, unroll):
    eye = eye_mask()
    place = lax.broadcasted_iota(jnp.int32, (targets, TILE), 0)

    def step(b, sums):
        products = products_of(b)
        residual = lane_sums(jnp.where(eye, rest[pl.ds(b, 1), :], 0.0) - products)
        lifted = jnp.sum(interp[b] * residual, axis=0, keepdims=True)
        return sums + jnp.where(place == owner[b] & (targets - 1), lifted, 0.0)

    return lax.fori_loop(0, count, step, jnp.zeros((targets, TILE), jnp.float32), unroll=unroll)


def diagonals(tiles, out, count, unroll):
    eye = eye_mask()

    def step(b, carry):
        out[pl.ds(b, 1), :] = jnp.sum(jnp.where(eye, tiles[b, 0], 0.0), axis=0, keepdims=True)
        return carry

    lax.fori_loop(0, count, step, 0, unroll=unroll)


def kernel(
    groups,
    rhs_hbm, tiles0_hbm, diag0_hbm, cols0_hbm, tiles1_hbm, diag1_hbm, cols1_hbm,
    tiles2_hbm, diag2_hbm, cols2_hbm, interp0_hbm, owner0_hbm, interp1_hbm, owner1_hbm,
    out0, out1, out2,
    rhs, tiles0, diag0, cols0, tiles1, diag1, cols1,
    tiles2, diag2, cols2, interp0, owner0, interp1, owner1,
    scale0, scale1, scale2, rest0, rest1, field2,
    fine_a, fine_b, fine_c, fine_d, mid_s, mid_a, mid_b, mid_c, mid_d,
    partial, parts, near, far,
    load_sem, send_sem, recv_sem,
):
    devices = groups * ROWS
    planes = groups // 2
    device, group, row = position()
    core = lax.rem(group, 2)
    plane = lax.div(group, 2)

    base0 = pl.multiple_of(lax.rem(device * R0, RING), R0)
    base1 = pl.multiple_of(lax.rem(device * R1, RING), R1)
    own0, own1 = pl.ds(base0, R0), pl.ds(base1, R1)

    own_tiles = pl.ds(0, 1)
    other_tiles = pl.ds(1, KN)

    def load(index, source, target):
        return pltpu.make_async_copy(source, target, load_sem.at[index])

    first = [
        load(0, tiles0_hbm.at[:, own_tiles], tiles0.at[:, own_tiles]),
        load(1, diag0_hbm, diag0),
        load(2, rhs_hbm, rhs),
    ]
    fine = [
        load(3, cols0_hbm, cols0),
        load(4, tiles0_hbm.at[:, other_tiles], tiles0.at[:, other_tiles]),
    ]
    middle = [
        load(5, tiles1_hbm, tiles1),
        load(6, diag1_hbm, diag1),
        load(7, cols1_hbm, cols1),
        load(8, interp0_hbm, interp0),
        load(9, owner0_hbm, owner0),
    ]
    coarse = [
        load(10, interp1_hbm, interp1),
        load(11, owner1_hbm, owner1),
        load(12, tiles2_hbm, tiles2),
        load(13, diag2_hbm, diag2),
        load(14, cols2_hbm, cols2),
    ]
    for copy in first:
        copy.start()

    mates = [(group, lax.rem(row + step, ROWS)) for step in range(1, ROWS)]
    far_peers = plane_peers(group, row, planes)
    after, before = lax.rem(group + 1, groups), lax.rem(group + groups - 1, groups)
    has_after, has_before = group < groups - 1, group > 0
    inside = jnp.logical_and(has_after, has_before)
    barrier = pltpu.get_barrier_semaphore()

    def greet(peers):
        for peer in peers:
            pl.semaphore_signal(barrier, inc=1, device_id=peer, device_id_type=MESH)

    @pl.when(has_after)
    def _():
        greet([(after, place) for place in range(ROWS)])

    @pl.when(has_before)
    def _():
        greet([(before, place) for place in range(ROWS)])

    greet(mates + far_peers)
    greeted = len(mates + far_peers) + jnp.where(has_after, ROWS, 0) + jnp.where(has_before, ROWS, 0)

    for copy in first:
        copy.wait()
    for copy in fine:
        copy.start()

    def send(index, source, target, peer):
        pltpu.make_async_remote_copy(
            src_ref=source, dst_ref=target, send_sem=send_sem.at[index], recv_sem=recv_sem.at[index],
            device_id=peer, device_id_type=MESH,
        ).start()

    def arrivals(index, like):
        return pltpu.make_async_remote_copy(
            src_ref=like, dst_ref=like, send_sem=send_sem.at[index], recv_sem=recv_sem.at[index],
            device_id=mates[0], device_id_type=MESH,
        )

    def exists(step):
        return device < devices - step if step > 0 else device >= -step

    def exchange(index, field, own, steps, rows):
        mine, reach = field.at[own], max(steps)
        interior = jnp.logical_and(exists(reach), exists(-reach))

        def post(step):
            send(index, mine, mine, along(device, step, devices))

        @pl.when(interior)
        def _():
            for step in steps:
                post(step)

        @pl.when(jnp.logical_not(interior))
        def _():
            for step in steps:
                pl.when(exists(step))(functools.partial(post, step))

        def await_all(wait):
            def several(count):
                wait(arrivals(index, field.at[pl.ds(0, rows * count)]))

            pl.when(interior)(functools.partial(several, 2 * reach))
            for place in range(reach):
                outer = jnp.logical_or(device == place, device == devices - 1 - place)
                pl.when(outer)(functools.partial(several, reach + place))

        finish.append(lambda: await_all(lambda copies: copies.wait_send()))
        return lambda: await_all(lambda copies: copies.wait_recv())

    def exchange_fine(index, field):
        return exchange(index, field, own0, (1, -1), R0)

    def exchange_middle(index, field):
        return exchange(index, field, own1, STEPS, R1)

    finish = []

    diagonals(tiles0, scale0, R0, 4)
    scale0[...] = relax / (diag0[...] + scale0[...])
    fine_a[own0, :] = rhs[...] * scale0[...]
    pl.semaphore_wait(barrier, greeted)
    fine_a_here = exchange_fine(0, fine_a)

    def rest_of(right, diag, tiles, field, own, count, unroll):
        mine = block_rows(own_products(tiles, field, own.start), count, unroll)
        return right - diag[...] * field[own, :] - mine

    def sweep0(field, here):
        started = field[own0, :] + scale0[...] * rest_of(rhs[...], diag0, tiles0, field, own0, R0, 16)
        here()
        return started - scale0[...] * block_rows(neighbour_products(tiles0, field, cols0), R0, 16)

    for copy in fine:
        copy.wait()
    for copy in middle + coarse:
        copy.start()
    fine_b[own0, :] = sweep0(fine_a, fine_a_here)
    fine_b_here = exchange_fine(2, fine_b)
    rest0[...] = rest_of(rhs[...], diag0, tiles0, fine_b, own0, R0, 16)
    for copy in middle:
        copy.wait()
    diagonals(tiles1, scale1, R1, 8)
    mid_s[own1, :] = relax / (diag1[...] + scale1[...])
    mid_s_here = exchange_middle(1, mid_s)
    fine_b_here()
    part = restrict(neighbour_products(tiles0, fine_b, cols0), rest0, interp0, owner0, R0, R0, 8)

    partial[...] = part
    slot = row * (3 * R0)
    parts[pl.ds(slot + R0, R0), :] = part

    @pl.when(has_after)
    def _():
        for place in range(ROWS):
            low = R1 * place
            send(3, partial.at[pl.ds(low, R0 - low)], parts.at[pl.ds(slot + low, R0 - low)], (after, place))

    @pl.when(has_before)
    def _():
        for place in range(ROWS):
            low = R1 * place
            send(3, partial.at[pl.ds(0, low + R1)], parts.at[pl.ds(slot + 2 * R0, low + R1)], (before, place))

    for mate in mates:
        send(3, partial, parts.at[pl.ds(slot + R0, R0)], mate)

    mate_rows = (ROWS - 1) * R0

    def parts_received():
        @pl.when(inside)
        def _():
            arrivals(3, parts.at[pl.ds(0, mate_rows + ROWS * (R0 + R1))]).wait_recv()

        for place in range(ROWS):
            @pl.when(jnp.logical_and(jnp.logical_not(has_before), row == place))
            def _():
                arrivals(3, parts.at[pl.ds(0, mate_rows + ROWS * R1 * (place + 1))]).wait_recv()

            @pl.when(jnp.logical_and(jnp.logical_not(has_after), row == place))
            def _():
                arrivals(3, parts.at[pl.ds(0, mate_rows + ROWS * (R0 - R1 * place))]).wait_recv()

    def parts_sent():
        one_side = sum(R1 * (place + 1) for place in range(ROWS))
        for sides, there in ((2, inside), (1, jnp.logical_not(inside))):
            @pl.when(there)
            def _():
                arrivals(3, parts.at[pl.ds(0, mate_rows + sides * one_side)]).wait_send()

    finish.append(parts_sent)
    mid_s_here()
    parts_received()
    for block in range(2 * ROWS + 1):
        offset = (row + block) * R1
        right = parts[pl.ds(offset, R1), :]
        for place in range(1, ROWS):
            right = right + parts[pl.ds(offset + place * 3 * R0, R1), :]
        there = pl.ds(pl.multiple_of(lax.rem((device + (devices + block - ROWS)) * R1, RING), R1), R1)
        mid_a[there, :] = right * mid_s[there, :]
        if block == ROWS:
            right1 = right
    s1 = mid_s[own1, :]

    v = mid_a[own1, :]
    mid_b[own1, :] = v + s1 * (
        right1 - diag1[...] * v - block_rows(all_products(tiles1, mid_a, cols1, base1), R1, 8)
    )
    mid_b_here = exchange_middle(4, mid_b)
    rest1[...] = rest_of(right1, diag1, tiles1, mid_b, own1, R1, 8)
    for copy in coarse:
        copy.wait()
    diagonals(tiles2, scale2, NB2, 8)
    scale2[...] = relax / (diag2[...] + scale2[...])
    mid_b_here()
    part2 = restrict(neighbour_products(tiles1, mid_b, cols1), rest1, interp1, owner1, R1, NB2, 8)

    line_slot = core * ROWS + row
    near[line_slot] = part2
    for peer in chip_line_peers(group, row):
        send(5, near.at[line_slot], near.at[line_slot], peer)
    arrivals(5, near.at[pl.ds(0, 2 * ROWS - 1)]).wait_recv()
    total = near[0]
    for place in range(1, 2 * ROWS):
        total = total + near[place]
    far[plane] = total
    for peer in far_peers:
        send(6, far.at[plane], far.at[plane], peer)
    arrivals(6, far.at[pl.ds(0, planes - 1)]).wait_recv()
    right2 = far[0]
    for place in range(1, planes):
        right2 = right2 + far[place]

    v2 = right2 * scale2[...]
    field2[...] = v2
    product2 = block_rows(all_products(tiles2, field2, cols2, 0), NB2, 16)
    v2 = v2 + scale2[...] * (right2 - diag2[...] * v2 - product2)
    out2[...] = v2

    def sweep1(field, here):
        started = field[own1, :] + s1 * rest_of(right1, diag1, tiles1, field, own1, R1, 8)
        here()
        return started - s1 * block_rows(neighbour_products(tiles1, field, cols1), R1, 8)

    mid_c[own1, :] = mid_b[own1, :] + prolong(interp1, out2, owner1, R1, 8)
    mid_c_here = exchange_middle(7, mid_c)
    mid_d[own1, :] = sweep1(mid_c, mid_c_here)
    mid_d_here = exchange_middle(8, mid_d)
    place1 = pl.ds(row * R1, R1)
    out1[place1, :] = sweep1(mid_d, mid_d_here)
    for mate in mates:
        send(9, out1.at[place1], out1.at[place1], mate)
    arrivals(9, out1.at[pl.ds(0, R0 - R1)]).wait_recv()

    fine_c[own0, :] = fine_b[own0, :] + prolong(interp0, out1, owner0, R0, 16)
    fine_c_here = exchange_fine(10, fine_c)
    fine_d[own0, :] = sweep0(fine_c, fine_c_here)
    fine_d_here = exchange_fine(11, fine_d)
    out0[...] = sweep0(fine_d, fine_d_here)

    for sent in finish:
        sent()
    for index, like in (
        (5, near.at[pl.ds(0, 2 * ROWS - 1)]), (6, far.at[pl.ds(0, planes - 1)]), (9, out1.at[pl.ds(0, R0 - R1)]),
    ):
        arrivals(index, like).wait_send()


def hand_over(*refs):
    sources, targets, sems = refs[:3], refs[3:6], refs[6]
    copies = [pltpu.make_async_copy(sources[i], targets[i], sems.at[i]) for i in range(3)]
    for copy in copies:
        copy.start()
    for copy in copies:
        copy.wait()


def shards(groups, *arguments):
    f32 = jnp.float32
    arguments = [a.T if a.dtype == jnp.int32 and a.ndim == 2 else a for a in arguments]
    vmem = lambda *shape: pltpu.VMEM(shape, f32)
    copies = []
    for index, argument in enumerate(arguments):
        space = pltpu.SMEM if argument.dtype == jnp.int32 else pltpu.VMEM
        copies.append(space(argument.shape, argument.dtype))
    scratch = copies + [
        vmem(R0, TILE), vmem(R1, TILE), vmem(NB2, TILE), vmem(R0, TILE), vmem(R1, TILE), vmem(NB2, TILE),
        *(vmem(RING, TILE) for _ in range(9)),
        vmem(R0, TILE), vmem(ROWS * 3 * R0, TILE), vmem(2 * ROWS, NB2, TILE), vmem(groups // 2, NB2, TILE),
        pltpu.SemaphoreType.DMA((16,)), pltpu.SemaphoreType.DMA((12,)), pltpu.SemaphoreType.DMA((12,)),
    ]
    out_shape = tuple(jax.ShapeDtypeStruct((n, TILE), f32) for n in (R0, R0, NB2))
    results = pl.pallas_call(
        functools.partial(kernel, groups),
        out_shape=tuple(vmem(n, TILE) for n in (R0, R0, NB2)),
        in_specs=[pl.BlockSpec(memory_space=pltpu.HBM)] * len(arguments),
        out_specs=(pl.BlockSpec(memory_space=pltpu.VMEM),) * 3,
        scratch_shapes=scratch,
        compiler_params=pltpu.CompilerParams(
            collective_id=0, has_side_effects=True, vmem_limit_bytes=56 * 2**20
        ),
        name="vcycle",
    )(*arguments)
    return pl.pallas_call(
        hand_over,
        out_shape=out_shape,
        in_specs=[pl.BlockSpec(memory_space=pl.ANY)] * 3,
        out_specs=(pl.BlockSpec(memory_space=pltpu.HBM),) * 3,
        scratch_shapes=[pltpu.SemaphoreType.DMA((3,))],
        compiler_params=pltpu.CompilerParams(vmem_limit_bytes=2**20),
        name="results",
    )(*results)


def solution(mesh):
    both = ("wa", "row")
    in_specs = (
        P(both, None),
        P(both, None, None, None),
        P(both, None),
        P(both, None),
        P(both, None, None, None),
        P(both, None),
        P(both, None),
        P(),
        P(),
        P(),
        P(both, None, None),
        P(both),
        P(both, None, None),
        P(both),
    )
    out_specs = (P(both, None), P("wa", None), P())
    return jax.shard_map(
        functools.partial(shards, mesh.shape["wa"]), mesh=mesh, in_specs=in_specs, out_specs=out_specs, check_vma=False
    )
```

```python
import functools

import jax
import jax.numpy as jnp
from jax import lax
from jax.experimental import pallas as pl
from jax.experimental.pallas import tpu as pltpu
from jax.sharding import PartitionSpec as P

MESH = pl.DeviceIdType.MESH
TILE = 128
KN = 4
R0 = 32
R1 = 8
NB2 = 16
ROWS = 4
RING = 128
relax = 0.8


def position():
    group, row = lax.axis_index("wa"), lax.axis_index("row")
    return group * ROWS + row, group, row


def along(device, offset, count):
    place = lax.rem(device + (offset + count), count)
    return lax.div(place, ROWS), lax.rem(place, ROWS)


STEPS = (2, -2, 1, -1, 3, -3, 4, -4)


def plane_peers(group, row, planes):
    plane, core = lax.div(group, 2), lax.rem(group, 2)
    return [(lax.rem(plane + step, planes) * 2 + core, row) for step in range(1, planes)]


def chip_line_peers(group, row):
    core = lax.rem(group, 2)
    out = []
    for step in range(1, 2 * ROWS):
        flip, shift = divmod(step, ROWS)
        out.append((group - core + lax.rem(core + flip, 2), lax.rem(row + shift, ROWS)))
    return out


def lane_sums(products):
    return jnp.sum(products, axis=1, keepdims=True)


def eye_mask():
    shape = (TILE, TILE)
    return lax.broadcasted_iota(jnp.int32, shape, 0) == lax.broadcasted_iota(jnp.int32, shape, 1)


def lanes():
    return lax.broadcasted_iota(jnp.int32, (TILE, TILE), 1)


def block_rows(products, count, unroll):
    lane = lanes()

    def step(b, columns):
        return jnp.where(lane == b, lane_sums(products(b)), columns)

    columns = lax.fori_loop(0, count, step, jnp.zeros((TILE, TILE), jnp.float32), unroll=unroll)
    return columns.T[:count]


def own_products(tiles, field, own):
    return lambda b: tiles[b, 0] * field[pl.ds(own + b, 1), :]


def neighbour_products(tiles, field, cols):
    last = field.shape[0] - 1

    def products(b):
        total = tiles[b, 1] * field[pl.ds(cols[0, b] & last, 1), :]
        for k in range(1, KN):
            total = total + tiles[b, k + 1] * field[pl.ds(cols[k, b] & last, 1), :]
        return total

    return products


def all_products(tiles, field, cols, own):
    mine, others = own_products(tiles, field, own), neighbour_products(tiles, field, cols)
    return lambda b: mine(b) + others(b)


def prolong(interp, coarse, owner, count, unroll):
    last = coarse.shape[0] - 1
    return block_rows(lambda b: interp[b] * coarse[pl.ds(owner[b] & last, 1), :], count, unroll)


def restrict(residual_of, interp, owner, count, targets, unroll):
    place = lax.broadcasted_iota(jnp.int32, (targets, TILE), 0)

    def step(b, sums):
        lifted = jnp.sum(interp[b] * residual_of(b), axis=0, keepdims=True)
        return sums + jnp.where(place == owner[b] & (targets - 1), lifted, 0.0)

    return lax.fori_loop(0, count, step, jnp.zeros((targets, TILE), jnp.float32), unroll=unroll)


def as_columns(rows):
    eye = eye_mask()
    return lambda b: lane_sums(jnp.where(eye, rows[pl.ds(b, 1), :], 0.0))


def summed(products):
    return lambda b: lane_sums(products(b))


def diagonals(tiles, out, count, unroll):
    eye = eye_mask()

    def step(b, carry):
        out[pl.ds(b, 1), :] = jnp.sum(jnp.where(eye, tiles[b, 0], 0.0), axis=0, keepdims=True)
        return carry

    lax.fori_loop(0, count, step, 0, unroll=unroll)


def kernel(
    groups,
    rhs_hbm, tiles0_hbm, diag0_hbm, cols0_hbm, tiles1_hbm, diag1_hbm, cols1_hbm,
    tiles2_hbm, diag2_hbm, cols2_hbm, interp0_hbm, owner0_hbm, interp1_hbm, owner1_hbm,
    out0, out1, out2,
    rhs, tiles0, diag0, cols0, tiles1, diag1, cols1,
    tiles2, diag2, cols2, interp0, owner0, interp1, owner1,
    scale0, scale1, scale2, rest0, rest1, rest2, field2, picked2,
    fine_a, fine_b, fine_c, fine_d, mid_s, mid_a, mid_b, mid_c, mid_d,
    partial, parts, near, far,
    load_sem, send_sem, recv_sem,
):
    devices = groups * ROWS
    planes = groups // 2
    device, group, row = position()
    core = lax.rem(group, 2)
    plane = lax.div(group, 2)

    base0 = pl.multiple_of(lax.rem(device * R0, RING), R0)
    base1 = pl.multiple_of(lax.rem(device * R1, RING), R1)
    own0, own1 = pl.ds(base0, R0), pl.ds(base1, R1)

    own_tiles = pl.ds(0, 1)
    other_tiles = pl.ds(1, KN)

    def load(index, source, target):
        return pltpu.make_async_copy(source, target, load_sem.at[index])

    first = [
        load(0, tiles0_hbm.at[:, own_tiles], tiles0.at[:, own_tiles]),
        load(1, diag0_hbm, diag0),
        load(2, rhs_hbm, rhs),
    ]
    fine = [
        load(3, cols0_hbm, cols0),
        load(4, tiles0_hbm.at[:, other_tiles], tiles0.at[:, other_tiles]),
    ]
    middle = [
        load(5, tiles1_hbm, tiles1),
        load(6, diag1_hbm, diag1),
        load(7, cols1_hbm, cols1),
        load(8, interp0_hbm, interp0),
        load(9, owner0_hbm, owner0),
    ]
    coarse = [
        load(10, interp1_hbm, interp1),
        load(11, owner1_hbm, owner1),
        load(12, tiles2_hbm, tiles2),
        load(13, diag2_hbm, diag2),
        load(14, cols2_hbm, cols2),
    ]
    mates = [(group, lax.rem(row + step, ROWS)) for step in range(1, ROWS)]
    far_peers = plane_peers(group, row, planes)
    after, before = lax.rem(group + 1, groups), lax.rem(group + groups - 1, groups)
    has_after, has_before = group < groups - 1, group > 0
    inside = jnp.logical_and(has_after, has_before)
    barrier = pltpu.get_barrier_semaphore()

    def greet(peers):
        for peer in peers:
            pl.semaphore_signal(barrier, inc=1, device_id=peer, device_id_type=MESH)

    @pl.when(has_after)
    def _():
        greet([(after, place) for place in range(ROWS)])

    @pl.when(has_before)
    def _():
        greet([(before, place) for place in range(ROWS)])

    for copy in first:
        copy.start()
    greet(mates + far_peers)
    greeted = len(mates + far_peers) + jnp.where(has_after, ROWS, 0) + jnp.where(has_before, ROWS, 0)

    for copy in first:
        copy.wait()
    for copy in fine:
        copy.start()

    def send(index, source, target, peer):
        pltpu.make_async_remote_copy(
            src_ref=source, dst_ref=target, send_sem=send_sem.at[index], recv_sem=recv_sem.at[index],
            device_id=peer, device_id_type=MESH,
        ).start()

    def arrivals(index, like):
        return pltpu.make_async_remote_copy(
            src_ref=like, dst_ref=like, send_sem=send_sem.at[index], recv_sem=recv_sem.at[index],
            device_id=mates[0], device_id_type=MESH,
        )

    def exists(step):
        return device < devices - step if step > 0 else device >= -step

    def exchange(index, field, own, steps, rows):
        mine, reach = field.at[own], max(steps)
        interior = jnp.logical_and(exists(reach), exists(-reach))

        def post(step):
            send(index, mine, mine, along(device, step, devices))

        @pl.when(interior)
        def _():
            for step in steps:
                post(step)

        @pl.when(jnp.logical_not(interior))
        def _():
            for step in steps:
                pl.when(exists(step))(functools.partial(post, step))

        def await_all(wait):
            def several(count):
                wait(arrivals(index, field.at[pl.ds(0, rows * count)]))

            pl.when(interior)(functools.partial(several, 2 * reach))
            for place in range(reach):
                outer = jnp.logical_or(device == place, device == devices - 1 - place)
                pl.when(outer)(functools.partial(several, reach + place))

        finish.append(lambda: await_all(lambda copies: copies.wait_send()))
        return lambda: await_all(lambda copies: copies.wait_recv())

    def exchange_fine(index, field):
        return exchange(index, field, own0, (1, -1), R0)

    def exchange_middle(index, field):
        return exchange(index, field, own1, STEPS, R1)

    finish = []

    diagonals(tiles0, scale0, R0, 4)
    scale0[...] = relax / (diag0[...] + scale0[...])
    fine_a[own0, :] = rhs[...] * scale0[...]
    pl.semaphore_wait(barrier, greeted)
    fine_a_here = exchange_fine(0, fine_a)

    def rest_of(right, diag, tiles, field, own, count, unroll):
        mine = block_rows(own_products(tiles, field, own.start), count, unroll)
        return right - diag[...] * field[own, :] - mine

    def sweep0(field, here):
        started = field[own0, :] + scale0[...] * rest_of(rhs[...], diag0, tiles0, field, own0, R0, 16)
        here()
        return started - scale0[...] * block_rows(neighbour_products(tiles0, field, cols0), R0, 32)

    for copy in fine:
        copy.wait()
    for copy in middle + coarse:
        copy.start()
    fine_b[own0, :] = sweep0(fine_a, fine_a_here)
    fine_b_here = exchange_fine(2, fine_b)
    for copy in middle:
        copy.wait()
    diagonals(tiles1, scale1, R1, 8)
    mid_s[own1, :] = relax / (diag1[...] + scale1[...])
    mid_s_here = exchange_middle(1, mid_s)
    rest0[...] = rest_of(rhs[...], diag0, tiles0, fine_b, own0, R0, 16)
    part = restrict(as_columns(rest0), interp0, owner0, R0, R0, 8)
    fine_b_here()
    part = part - restrict(summed(neighbour_products(tiles0, fine_b, cols0)), interp0, owner0, R0, R0, 16)

    partial[...] = part
    slot = row * (3 * R0)
    parts[pl.ds(slot + R0, R0), :] = part

    @pl.when(has_after)
    def _():
        for place in range(ROWS):
            low = R1 * place
            send(3, partial.at[pl.ds(low, R0 - low)], parts.at[pl.ds(slot + low, R0 - low)], (after, place))

    @pl.when(has_before)
    def _():
        for place in range(ROWS):
            low = R1 * place
            send(3, partial.at[pl.ds(0, low + R1)], parts.at[pl.ds(slot + 2 * R0, low + R1)], (before, place))

    for mate in mates:
        send(3, partial, parts.at[pl.ds(slot + R0, R0)], mate)

    mate_rows = (ROWS - 1) * R0

    def parts_received():
        @pl.when(inside)
        def _():
            arrivals(3, parts.at[pl.ds(0, mate_rows + ROWS * (R0 + R1))]).wait_recv()

        for place in range(ROWS):
            @pl.when(jnp.logical_and(jnp.logical_not(has_before), row == place))
            def _():
                arrivals(3, parts.at[pl.ds(0, mate_rows + ROWS * R1 * (place + 1))]).wait_recv()

            @pl.when(jnp.logical_and(jnp.logical_not(has_after), row == place))
            def _():
                arrivals(3, parts.at[pl.ds(0, mate_rows + ROWS * (R0 - R1 * place))]).wait_recv()

    def parts_sent():
        one_side = sum(R1 * (place + 1) for place in range(ROWS))
        for sides, there in ((2, inside), (1, jnp.logical_not(inside))):
            @pl.when(there)
            def _():
                arrivals(3, parts.at[pl.ds(0, mate_rows + sides * one_side)]).wait_send()

    finish.append(parts_sent)
    mid_s_here()
    parts_received()
    for block in range(2 * ROWS + 1):
        offset = (row + block) * R1
        right = parts[pl.ds(offset, R1), :]
        for place in range(1, ROWS):
            right = right + parts[pl.ds(offset + place * 3 * R0, R1), :]
        there = pl.ds(pl.multiple_of(lax.rem((device + (devices + block - ROWS)) * R1, RING), R1), R1)
        mid_a[there, :] = right * mid_s[there, :]
        if block == ROWS:
            right1 = right
    s1 = mid_s[own1, :]

    v = mid_a[own1, :]
    mid_b[own1, :] = v + s1 * (
        right1 - diag1[...] * v - block_rows(all_products(tiles1, mid_a, cols1, base1), R1, 8)
    )
    mid_b_here = exchange_middle(4, mid_b)
    for copy in coarse:
        copy.wait()
    rest1[...] = rest_of(right1, diag1, tiles1, mid_b, own1, R1, 8)
    part2 = restrict(as_columns(rest1), interp1, owner1, R1, NB2, 8)
    diagonals(tiles2, scale2, NB2, 8)
    scale2[...] = relax / (diag2[...] + scale2[...])
    mid_b_here()

    line_slot = core * ROWS + row
    near[line_slot] = part2 - restrict(
        summed(neighbour_products(tiles1, mid_b, cols1)), interp1, owner1, R1, NB2, 8
    )
    for peer in chip_line_peers(group, row):
        send(5, near.at[line_slot], near.at[line_slot], peer)
    arrivals(5, near.at[pl.ds(0, 2 * ROWS - 1)]).wait_recv()
    total = near[0]
    for place in range(1, 2 * ROWS):
        total = total + near[place]
    far[plane] = total
    for peer in far_peers:
        send(6, far.at[plane], far.at[plane], peer)
    arrivals(6, far.at[pl.ds(0, planes - 1)]).wait_recv()
    right2 = far[0]
    for place in range(1, planes):
        right2 = right2 + far[place]

    v2 = right2 * scale2[...]
    field2[...] = v2
    rest2[...] = v2 + scale2[...] * (right2 - diag2[...] * v2)

    def coarse_products(b):
        return all_products(tiles2, field2, cols2, 0)(b)

    def owned(b):
        return owner1[b] & (NB2 - 1)

    product2 = block_rows(lambda b: coarse_products(owned(b)), R1, 8)
    for b in range(R1):
        here = pl.ds(owned(b), 1)
        picked2[pl.ds(b, 1), :] = rest2[here, :] - scale2[here, :] * product2[b:b + 1]
    mid_c[own1, :] = mid_b[own1, :] + block_rows(lambda b: interp1[b] * picked2[pl.ds(b, 1), :], R1, 8)
    mid_c_here = exchange_middle(7, mid_c)
    out2[...] = rest2[...] - scale2[...] * block_rows(coarse_products, NB2, 16)

    def sweep1(field, here):
        started = field[own1, :] + s1 * rest_of(right1, diag1, tiles1, field, own1, R1, 8)
        here()
        return started - s1 * block_rows(neighbour_products(tiles1, field, cols1), R1, 8)

    mid_d[own1, :] = sweep1(mid_c, mid_c_here)
    mid_d_here = exchange_middle(8, mid_d)
    place1 = pl.ds(row * R1, R1)
    out1[place1, :] = sweep1(mid_d, mid_d_here)
    for mate in mates:
        send(9, out1.at[place1], out1.at[place1], mate)
    arrivals(9, out1.at[pl.ds(0, R0 - R1)]).wait_recv()

    fine_c[own0, :] = fine_b[own0, :] + prolong(interp0, out1, owner0, R0, 16)
    fine_c_here = exchange_fine(10, fine_c)
    fine_d[own0, :] = sweep0(fine_c, fine_c_here)
    fine_d_here = exchange_fine(11, fine_d)
    out0[...] = sweep0(fine_d, fine_d_here)

    for sent in finish:
        sent()
    for index, like in (
        (5, near.at[pl.ds(0, 2 * ROWS - 1)]), (6, far.at[pl.ds(0, planes - 1)]), (9, out1.at[pl.ds(0, R0 - R1)]),
    ):
        arrivals(index, like).wait_send()


def hand_over(*refs):
    sources, targets, sems = refs[:3], refs[3:6], refs[6]
    copies = [pltpu.make_async_copy(sources[i], targets[i], sems.at[i]) for i in range(3)]
    for copy in copies:
        copy.start()
    for copy in copies:
        copy.wait()


def shards(groups, *arguments):
    f32 = jnp.float32
    arguments = [a.T if a.dtype == jnp.int32 and a.ndim == 2 else a for a in arguments]
    vmem = lambda *shape: pltpu.VMEM(shape, f32)
    copies = []
    for index, argument in enumerate(arguments):
        space = pltpu.SMEM if argument.dtype == jnp.int32 else pltpu.VMEM
        copies.append(space(argument.shape, argument.dtype))
    scratch = copies + [
        vmem(R0, TILE), vmem(R1, TILE), vmem(NB2, TILE), vmem(R0, TILE), vmem(R1, TILE), vmem(NB2, TILE),
        vmem(NB2, TILE), vmem(R1, TILE),
        *(vmem(RING, TILE) for _ in range(9)),
        vmem(R0, TILE), vmem(ROWS * 3 * R0, TILE),
        vmem(2 * ROWS, NB2, TILE), vmem(groups // 2, NB2, TILE),
        pltpu.SemaphoreType.DMA((16,)), pltpu.SemaphoreType.DMA((12,)), pltpu.SemaphoreType.DMA((12,)),
    ]
    out_shape = tuple(jax.ShapeDtypeStruct((n, TILE), f32) for n in (R0, R0, NB2))
    results = pl.pallas_call(
        functools.partial(kernel, groups),
        out_shape=tuple(vmem(n, TILE) for n in (R0, R0, NB2)),
        in_specs=[pl.BlockSpec(memory_space=pltpu.HBM)] * len(arguments),
        out_specs=(pl.BlockSpec(memory_space=pltpu.VMEM),) * 3,
        scratch_shapes=scratch,
        compiler_params=pltpu.CompilerParams(
            collective_id=0, has_side_effects=True, vmem_limit_bytes=56 * 2**20
        ),
        name="vcycle",
    )(*arguments)
    return pl.pallas_call(
        hand_over,
        out_shape=out_shape,
        in_specs=[pl.BlockSpec(memory_space=pl.ANY)] * 3,
        out_specs=(pl.BlockSpec(memory_space=pltpu.HBM),) * 3,
        scratch_shapes=[pltpu.SemaphoreType.DMA((3,))],
        compiler_params=pltpu.CompilerParams(vmem_limit_bytes=2**20),
        name="results",
    )(*results)


def solution(mesh):
    both = ("wa", "row")
    in_specs = (
        P(both, None),
        P(both, None, None, None),
        P(both, None),
        P(both, None),
        P(both, None, None, None),
        P(both, None),
        P(both, None),
        P(),
        P(),
        P(),
        P(both, None, None),
        P(both),
        P(both, None, None),
        P(both),
    )
    out_specs = (P(both, None), P("wa", None), P())
    return jax.shard_map(
        functools.partial(shards, mesh.shape["wa"]), mesh=mesh, in_specs=in_specs, out_specs=out_specs, check_vma=False
    )
```

```python
import functools

import jax
import jax.numpy as jnp
from jax import lax
from jax.experimental import pallas as pl
from jax.experimental.pallas import tpu as pltpu
from jax.sharding import PartitionSpec as P

MESH = pl.DeviceIdType.MESH
TILE = 128
KN = 4
R0 = 32
R1 = 8
NB2 = 16
ROWS = 4
RING = 128
relax = 0.8


def position():
    group, row = lax.axis_index("wa"), lax.axis_index("row")
    return group * ROWS + row, group, row


def along(device, offset, count):
    place = lax.rem(device + (offset + count), count)
    return lax.div(place, ROWS), lax.rem(place, ROWS)


STEPS = (2, -2, 1, -1, 3, -3, 4, -4)


def plane_peers(group, row, planes):
    plane, core = lax.div(group, 2), lax.rem(group, 2)
    return [(lax.rem(plane + step, planes) * 2 + core, row) for step in range(1, planes)]


def chip_line_peers(group, row):
    core = lax.rem(group, 2)
    out = []
    for step in range(1, 2 * ROWS):
        flip, shift = divmod(step, ROWS)
        out.append((group - core + lax.rem(core + flip, 2), lax.rem(row + shift, ROWS)))
    return out


def lane_sums(products):
    return jnp.sum(products, axis=1, keepdims=True)


def eye_mask():
    shape = (TILE, TILE)
    return lax.broadcasted_iota(jnp.int32, shape, 0) == lax.broadcasted_iota(jnp.int32, shape, 1)


def lanes():
    return lax.broadcasted_iota(jnp.int32, (TILE, TILE), 1)


def block_rows(products, count, unroll):
    lane = lanes()

    def step(b, columns):
        return jnp.where(lane == b, lane_sums(products(b)), columns)

    columns = lax.fori_loop(0, count, step, jnp.zeros((TILE, TILE), jnp.float32), unroll=unroll)
    return columns.T[:count]


def own_products(tiles, field, own):
    return lambda b: tiles[b, 0] * field[pl.ds(own + b, 1), :]


def neighbour_products(tiles, field, cols):
    last = field.shape[0] - 1

    def products(b):
        total = tiles[b, 1] * field[pl.ds(cols[0, b] & last, 1), :]
        for k in range(1, KN):
            total = total + tiles[b, k + 1] * field[pl.ds(cols[k, b] & last, 1), :]
        return total

    return products


def all_products(tiles, field, cols, own):
    mine, others = own_products(tiles, field, own), neighbour_products(tiles, field, cols)
    return lambda b: mine(b) + others(b)


def prolong(interp, coarse, owner, count, unroll):
    last = coarse.shape[0] - 1
    return block_rows(lambda b: interp[b] * coarse[pl.ds(owner[b] & last, 1), :], count, unroll)


def restrict(residual_of, interp, owner, count, targets, unroll):
    place = lax.broadcasted_iota(jnp.int32, (targets, TILE), 0)

    def step(b, sums):
        lifted = jnp.sum(interp[b] * residual_of(b), axis=0, keepdims=True)
        return sums + jnp.where(place == owner[b] & (targets - 1), lifted, 0.0)

    return lax.fori_loop(0, count, step, jnp.zeros((targets, TILE), jnp.float32), unroll=unroll)


def as_columns(rows):
    eye = eye_mask()
    return lambda b: lane_sums(jnp.where(eye, rows[pl.ds(b, 1), :], 0.0))


def summed(products):
    return lambda b: lane_sums(products(b))


def diagonals(tiles, out, count, unroll):
    eye = eye_mask()

    def step(b, carry):
        out[pl.ds(b, 1), :] = jnp.sum(jnp.where(eye, tiles[b, 0], 0.0), axis=0, keepdims=True)
        return carry

    lax.fori_loop(0, count, step, 0, unroll=unroll)


def kernel(
    groups,
    rhs_hbm, tiles0_hbm, diag0_hbm, cols0_hbm, tiles1_hbm, diag1_hbm, cols1_hbm,
    tiles2_hbm, diag2_hbm, cols2_hbm, interp0_hbm, owner0_hbm, interp1_hbm, owner1_hbm,
    out0, out1, out2,
    rhs, tiles0, diag0, cols0, tiles1, diag1, cols1,
    tiles2, diag2, cols2, interp0, owner0, interp1, owner1,
    scale0, scale1, scale2, rest0, rest1, rest2, field2, picked2,
    fine_a, fine_b, fine_c, fine_d, mid_s, mid_a, mid_b, mid_c, mid_d,
    partial, parts, near, far,
    load_sem, send_sem, recv_sem,
):
    devices = groups * ROWS
    planes = groups // 2
    device, group, row = position()
    core = lax.rem(group, 2)
    plane = lax.div(group, 2)

    base0 = pl.multiple_of(lax.rem(device * R0, RING), R0)
    base1 = pl.multiple_of(lax.rem(device * R1, RING), R1)
    own0, own1 = pl.ds(base0, R0), pl.ds(base1, R1)

    own_tiles = pl.ds(0, 1)
    other_tiles = pl.ds(1, KN)

    def load(index, source, target):
        return pltpu.make_async_copy(source, target, load_sem.at[index])

    first = [
        load(0, tiles0_hbm.at[:, own_tiles], tiles0.at[:, own_tiles]),
        load(1, diag0_hbm, diag0),
        load(2, rhs_hbm, rhs),
    ]
    fine = [
        load(3, cols0_hbm, cols0),
        load(4, tiles0_hbm.at[:, other_tiles], tiles0.at[:, other_tiles]),
    ]
    middle = [
        load(5, tiles1_hbm, tiles1),
        load(6, diag1_hbm, diag1),
        load(7, cols1_hbm, cols1),
        load(8, interp0_hbm, interp0),
        load(9, owner0_hbm, owner0),
    ]
    coarse = [
        load(10, interp1_hbm, interp1),
        load(11, owner1_hbm, owner1),
        load(12, tiles2_hbm, tiles2),
        load(13, diag2_hbm, diag2),
        load(14, cols2_hbm, cols2),
    ]
    mates = [(group, lax.rem(row + step, ROWS)) for step in range(1, ROWS)]
    far_peers = plane_peers(group, row, planes)
    after, before = lax.rem(group + 1, groups), lax.rem(group + groups - 1, groups)
    has_after, has_before = group < groups - 1, group > 0
    inside = jnp.logical_and(has_after, has_before)
    barrier = pltpu.get_barrier_semaphore()

    def greet(peers):
        for peer in peers:
            pl.semaphore_signal(barrier, inc=1, device_id=peer, device_id_type=MESH)

    @pl.when(has_after)
    def _():
        greet([(after, place) for place in range(ROWS)])

    @pl.when(has_before)
    def _():
        greet([(before, place) for place in range(ROWS)])

    for copy in first:
        copy.start()
    greet(mates + far_peers)
    greeted = len(mates + far_peers) + jnp.where(has_after, ROWS, 0) + jnp.where(has_before, ROWS, 0)

    for copy in first:
        copy.wait()
    for copy in fine:
        copy.start()

    def send(index, source, target, peer):
        pltpu.make_async_remote_copy(
            src_ref=source, dst_ref=target, send_sem=send_sem.at[index], recv_sem=recv_sem.at[index],
            device_id=peer, device_id_type=MESH,
        ).start()

    def arrivals(index, like):
        return pltpu.make_async_remote_copy(
            src_ref=like, dst_ref=like, send_sem=send_sem.at[index], recv_sem=recv_sem.at[index],
            device_id=mates[0], device_id_type=MESH,
        )

    def exists(step):
        return device < devices - step if step > 0 else device >= -step

    def exchange(index, field, own, steps, rows):
        mine, reach = field.at[own], max(steps)
        interior = jnp.logical_and(exists(reach), exists(-reach))

        def post(step):
            send(index, mine, mine, along(device, step, devices))

        @pl.when(interior)
        def _():
            for step in steps:
                post(step)

        @pl.when(jnp.logical_not(interior))
        def _():
            for step in steps:
                pl.when(exists(step))(functools.partial(post, step))

        def await_all(wait):
            def several(count):
                wait(arrivals(index, field.at[pl.ds(0, rows * count)]))

            pl.when(interior)(functools.partial(several, 2 * reach))
            for place in range(reach):
                outer = jnp.logical_or(device == place, device == devices - 1 - place)
                pl.when(outer)(functools.partial(several, reach + place))

        finish.append(lambda: await_all(lambda copies: copies.wait_send()))
        return lambda: await_all(lambda copies: copies.wait_recv())

    def exchange_fine(index, field):
        return exchange(index, field, own0, (1, -1), R0)

    def exchange_middle(index, field):
        return exchange(index, field, own1, STEPS, R1)

    finish = []

    diagonals(tiles0, scale0, R0, 4)
    scale0[...] = relax / (diag0[...] + scale0[...])
    fine_a[own0, :] = rhs[...] * scale0[...]
    pl.semaphore_wait(barrier, greeted)
    fine_a_here = exchange_fine(0, fine_a)

    def rest_of(right, diag, tiles, field, own, count, unroll):
        mine = block_rows(own_products(tiles, field, own.start), count, unroll)
        return right - diag[...] * field[own, :] - mine

    def sweep0(field, here):
        started = field[own0, :] + scale0[...] * rest_of(rhs[...], diag0, tiles0, field, own0, R0, 16)
        here()
        return started - scale0[...] * block_rows(neighbour_products(tiles0, field, cols0), R0, 32)

    for copy in fine:
        copy.wait()
    for copy in middle + coarse:
        copy.start()
    fine_b[own0, :] = sweep0(fine_a, fine_a_here)
    fine_b_here = exchange_fine(2, fine_b)
    for copy in middle:
        copy.wait()
    diagonals(tiles1, scale1, R1, 8)
    mid_s[own1, :] = relax / (diag1[...] + scale1[...])
    mid_s_here = exchange_middle(1, mid_s)
    rest0[...] = rest_of(rhs[...], diag0, tiles0, fine_b, own0, R0, 16)
    part = restrict(as_columns(rest0), interp0, owner0, R0, R0, 8)
    fine_b_here()
    part = part - restrict(summed(neighbour_products(tiles0, fine_b, cols0)), interp0, owner0, R0, R0, 32)

    partial[...] = part
    slot = row * (3 * R0)
    parts[pl.ds(slot + R0, R0), :] = part

    @pl.when(has_after)
    def _():
        for place in range(ROWS):
            low = R1 * place
            send(3, partial.at[pl.ds(low, R0 - low)], parts.at[pl.ds(slot + low, R0 - low)], (after, place))

    @pl.when(has_before)
    def _():
        for place in range(ROWS):
            low = R1 * place
            send(3, partial.at[pl.ds(0, low + R1)], parts.at[pl.ds(slot + 2 * R0, low + R1)], (before, place))

    for mate in mates:
        send(3, partial, parts.at[pl.ds(slot + R0, R0)], mate)

    mate_rows = (ROWS - 1) * R0

    def parts_received():
        @pl.when(inside)
        def _():
            arrivals(3, parts.at[pl.ds(0, mate_rows + ROWS * (R0 + R1))]).wait_recv()

        for place in range(ROWS):
            @pl.when(jnp.logical_and(jnp.logical_not(has_before), row == place))
            def _():
                arrivals(3, parts.at[pl.ds(0, mate_rows + ROWS * R1 * (place + 1))]).wait_recv()

            @pl.when(jnp.logical_and(jnp.logical_not(has_after), row == place))
            def _():
                arrivals(3, parts.at[pl.ds(0, mate_rows + ROWS * (R0 - R1 * place))]).wait_recv()

    def parts_sent():
        one_side = sum(R1 * (place + 1) for place in range(ROWS))
        for sides, there in ((2, inside), (1, jnp.logical_not(inside))):
            @pl.when(there)
            def _():
                arrivals(3, parts.at[pl.ds(0, mate_rows + sides * one_side)]).wait_send()

    finish.append(parts_sent)
    mid_s_here()
    parts_received()
    for block in range(2 * ROWS + 1):
        offset = (row + block) * R1
        right = parts[pl.ds(offset, R1), :]
        for place in range(1, ROWS):
            right = right + parts[pl.ds(offset + place * 3 * R0, R1), :]
        there = pl.ds(pl.multiple_of(lax.rem((device + (devices + block - ROWS)) * R1, RING), R1), R1)
        mid_a[there, :] = right * mid_s[there, :]
        if block == ROWS:
            right1 = right
    s1 = mid_s[own1, :]

    v = mid_a[own1, :]
    mid_b[own1, :] = v + s1 * (
        right1 - diag1[...] * v - block_rows(all_products(tiles1, mid_a, cols1, base1), R1, 8)
    )
    mid_b_here = exchange_middle(4, mid_b)
    for copy in coarse:
        copy.wait()
    rest1[...] = rest_of(right1, diag1, tiles1, mid_b, own1, R1, 8)
    part2 = restrict(as_columns(rest1), interp1, owner1, R1, NB2, 8)
    diagonals(tiles2, scale2, NB2, 8)
    scale2[...] = relax / (diag2[...] + scale2[...])
    mid_b_here()

    line_slot = core * ROWS + row
    near[line_slot] = part2 - restrict(
        summed(neighbour_products(tiles1, mid_b, cols1)), interp1, owner1, R1, NB2, 8
    )
    for peer in chip_line_peers(group, row):
        send(5, near.at[line_slot], near.at[line_slot], peer)
    arrivals(5, near.at[pl.ds(0, 2 * ROWS - 1)]).wait_recv()
    total = near[0]
    for place in range(1, 2 * ROWS):
        total = total + near[place]
    far[plane] = total
    for peer in far_peers:
        send(6, far.at[plane], far.at[plane], peer)
    arrivals(6, far.at[pl.ds(0, planes - 1)]).wait_recv()
    right2 = far[0]
    for place in range(1, planes):
        right2 = right2 + far[place]

    v2 = right2 * scale2[...]
    field2[...] = v2
    rest2[...] = v2 + scale2[...] * (right2 - diag2[...] * v2)

    def coarse_products(b):
        return all_products(tiles2, field2, cols2, 0)(b)

    def owned(b):
        return owner1[b] & (NB2 - 1)

    product2 = block_rows(lambda b: coarse_products(owned(b)), R1, 8)
    for b in range(R1):
        here = pl.ds(owned(b), 1)
        picked2[pl.ds(b, 1), :] = rest2[here, :] - scale2[here, :] * product2[b:b + 1]
    mid_c[own1, :] = mid_b[own1, :] + block_rows(lambda b: interp1[b] * picked2[pl.ds(b, 1), :], R1, 8)
    mid_c_here = exchange_middle(7, mid_c)
    out2[...] = rest2[...] - scale2[...] * block_rows(coarse_products, NB2, 16)

    def sweep1(field, here):
        started = field[own1, :] + s1 * rest_of(right1, diag1, tiles1, field, own1, R1, 8)
        here()
        return started - s1 * block_rows(neighbour_products(tiles1, field, cols1), R1, 8)

    mid_d[own1, :] = sweep1(mid_c, mid_c_here)
    mid_d_here = exchange_middle(8, mid_d)
    place1 = pl.ds(row * R1, R1)
    out1[place1, :] = sweep1(mid_d, mid_d_here)
    for mate in mates:
        send(9, out1.at[place1], out1.at[place1], mate)
    arrivals(9, out1.at[pl.ds(0, R0 - R1)]).wait_recv()

    fine_c[own0, :] = fine_b[own0, :] + prolong(interp0, out1, owner0, R0, 32)
    fine_c_here = exchange_fine(10, fine_c)
    fine_d[own0, :] = sweep0(fine_c, fine_c_here)
    fine_d_here = exchange_fine(11, fine_d)
    out0[...] = sweep0(fine_d, fine_d_here)

    for sent in finish:
        sent()
    for index, like in (
        (5, near.at[pl.ds(0, 2 * ROWS - 1)]), (6, far.at[pl.ds(0, planes - 1)]), (9, out1.at[pl.ds(0, R0 - R1)]),
    ):
        arrivals(index, like).wait_send()


def hand_over(*refs):
    sources, targets, sems = refs[:3], refs[3:6], refs[6]
    copies = [pltpu.make_async_copy(sources[i], targets[i], sems.at[i]) for i in range(3)]
    for copy in copies:
        copy.start()
    for copy in copies:
        copy.wait()


def shards(groups, *arguments):
    f32 = jnp.float32
    arguments = [a.T if a.dtype == jnp.int32 and a.ndim == 2 else a for a in arguments]
    vmem = lambda *shape: pltpu.VMEM(shape, f32)
    copies = []
    for index, argument in enumerate(arguments):
        space = pltpu.SMEM if argument.dtype == jnp.int32 else pltpu.VMEM
        copies.append(space(argument.shape, argument.dtype))
    scratch = copies + [
        vmem(R0, TILE), vmem(R1, TILE), vmem(NB2, TILE), vmem(R0, TILE), vmem(R1, TILE), vmem(NB2, TILE),
        vmem(NB2, TILE), vmem(R1, TILE),
        *(vmem(RING, TILE) for _ in range(9)),
        vmem(R0, TILE), vmem(ROWS * 3 * R0, TILE),
        vmem(2 * ROWS, NB2, TILE), vmem(groups // 2, NB2, TILE),
        pltpu.SemaphoreType.DMA((16,)), pltpu.SemaphoreType.DMA((12,)), pltpu.SemaphoreType.DMA((12,)),
    ]
    out_shape = tuple(jax.ShapeDtypeStruct((n, TILE), f32) for n in (R0, R0, NB2))
    results = pl.pallas_call(
        functools.partial(kernel, groups),
        out_shape=tuple(vmem(n, TILE) for n in (R0, R0, NB2)),
        in_specs=[pl.BlockSpec(memory_space=pltpu.HBM)] * len(arguments),
        out_specs=(pl.BlockSpec(memory_space=pltpu.VMEM),) * 3,
        scratch_shapes=scratch,
        compiler_params=pltpu.CompilerParams(
            collective_id=0, has_side_effects=True, vmem_limit_bytes=56 * 2**20
        ),
        name="vcycle",
    )(*arguments)
    return pl.pallas_call(
        hand_over,
        out_shape=out_shape,
        in_specs=[pl.BlockSpec(memory_space=pl.ANY)] * 3,
        out_specs=(pl.BlockSpec(memory_space=pltpu.HBM),) * 3,
        scratch_shapes=[pltpu.SemaphoreType.DMA((3,))],
        compiler_params=pltpu.CompilerParams(vmem_limit_bytes=2**20),
        name="results",
    )(*results)


def solution(mesh):
    both = ("wa", "row")
    in_specs = (
        P(both, None),
        P(both, None, None, None),
        P(both, None),
        P(both, None),
        P(both, None, None, None),
        P(both, None),
        P(both, None),
        P(),
        P(),
        P(),
        P(both, None, None),
        P(both),
        P(both, None, None),
        P(both),
    )
    out_specs = (P(both, None), P("wa", None), P())
    return jax.shard_map(
        functools.partial(shards, mesh.shape["wa"]), mesh=mesh, in_specs=in_specs, out_specs=out_specs, check_vma=False
    )
```
